32 devices in a mesh: fiber: 2 (over x), chan: 16 (over z, y, core).
Axes of the slice: x: 2, y: 2, z: 4, core: 2. Of those that a mesh axis runs over, the one named last changes fastest.
Arguments:
- recording: bfloat16 [1024, 16384], P('fiber', 'chan'), parts along dimension 0, may hold values from -6 to 6
- source_index: int32 [1024], P('fiber'), parts along dimension 0, may hold values from 0 to 511
- channel_mask: int32 [1024], P(('fiber', 'chan')), parts along dimension 0, may hold values 0 or 1
Outputs:
- correlations: bfloat16 [1024, 512, 256], P('fiber', 'chan'), parts along dimension 0
The draws below stay inside these ranges and needn't reach their ends.
There are 2 independent parts, one for each index of `fiber`. The reference program is written for one: setup_inputs(seed, part) draws one part's arguments, and reference() takes and returns one part's arrays. A program takes and returns all parts, laid end to end along the dimension named above; each array names one. Nothing has to cross between parts.
Inputs may be any that keep to these rules, and one draw needn't show every extreme that they name: `source_index`: indices of virtual-source channels of this fiber; they may repeat and may name bad channels. `channel_mask`: one flag for each channel.
All inputs are finite; a program needn't handle non-finite values. No bound on the sum of `channel_mask` on one device may be relied on, other than what follows from the above.
Results may differ from the reference program's by a relative error of at most 0.0092.
Values may be sent and summed in bfloat16 or wider, within the bound.
A program may use at most 128 MiB of HBM per device.

```python
import math
import jax
import jax.numpy as jnp
from jax import lax

CH_DEV = 32
SEGS = 8
NSEG = 512
NF = 192
FBASE = 4
LAGS = 256
TAPS = 64
SOURCES = 512
CHANNELS = 512
NT = 4096
RAW = 16384
N_CHAN = 16


def set_ends(drawn, key, least, top_value):
    longest = drawn.shape.index(max(drawn.shape))
    spots = []
    for shift in (0, 1):
        where = [jax.random.randint(jax.random.fold_in(key, axis), (), 0, length) for axis, length in enumerate(drawn.shape)]
        where[longest] = (where[longest] + shift) % drawn.shape[longest]
        spots.append(tuple(where))
    return drawn.at[spots[0]].set(least).at[spots[1]].set(top_value)


def levels(stream_key, shape, shards, least, largest):
    loudness = 1.0
    for axis_at, blocks in shards:
        heights = jax.random.uniform(jax.random.fold_in(jax.random.fold_in(stream_key, 6), axis_at), (blocks,), jnp.float32, least / len(shards), largest / len(shards))
        loudness = loudness * jnp.repeat(jnp.exp(heights), shape[axis_at] // blocks).reshape((-1,) + (1,) * (len(shape) - 1 - axis_at))
    return loudness


def gaussian(stream_key, extent, scale, bound, split=(), kind=jnp.bfloat16):
    values = jax.random.normal(stream_key, extent, jnp.float32) * scale
    if len(split) > 0:
        values = levels(stream_key, extent, split, -0.22, 0.18) * values
    return jnp.clip(values, min=-bound, max=bound).astype(kind)


def setup_inputs(seed: int = 0, part: int = 0) -> dict:
    splits = jax.random.split(jax.random.key(seed), 4)
    part_keys = jax.random.split(jax.random.fold_in(splits[3], part), 4)
    recording = gaussian(part_keys[0], (CHANNELS, RAW), 1.0, 6.0, ((1, 16),))
    source_index = set_ends(jax.random.randint(part_keys[1], (SOURCES,), 0, CHANNELS), jax.random.fold_in(part_keys[1], 1), 0, CHANNELS - 1).astype(jnp.int32)
    channel_mask = set_ends((jax.random.randint(part_keys[2], (CHANNELS,), 0, 8) < 7).astype(jnp.int32), jax.random.fold_in(part_keys[2], 1), 0, 1)
    return {"recording": recording, "source_index": source_index, "channel_mask": channel_mask}


def lowpass_taps():
    offsets = jnp.arange(TAPS, dtype=jnp.float32) - (TAPS - 1) / 2.0
    cutoff = 0.1
    window = 0.5 - 0.5 * jnp.cos(2.0 * math.pi * (jnp.arange(TAPS, dtype=jnp.float32) + 0.5) / TAPS)
    kernel = 2.0 * cutoff * jnp.sinc(2.0 * cutoff * offsets) * window
    kernel = kernel / jnp.sum(kernel)
    return kernel[::-1].astype(jnp.bfloat16)

def decimate(padded, reversed_taps, out_length):
    summed = jnp.zeros((padded.shape[0], out_length), jnp.float32)
    for stride in range(TAPS // 4):
        window_rows = padded[:, 4 * stride:4 * stride + 4 * out_length].reshape(padded.shape[0], out_length, 4)
        weights = reversed_taps[4 * stride:4 * stride + 4]
        summed = summed + jnp.einsum('ctq,q->ct', window_rows.astype(jnp.float32), weights.astype(jnp.float32))
    return summed.astype(jnp.bfloat16)

def fourier_table():
    sample = jnp.arange(NSEG, dtype=jnp.int32)[:, None]
    frequency = FBASE + jnp.arange(NF, dtype=jnp.int32)[None, :]
    angles = 2.0 * math.pi * (sample * frequency % NSEG).astype(jnp.float32) / NSEG
    return jnp.concatenate([jnp.cos(angles), -jnp.sin(angles)], axis=1).astype(jnp.bfloat16)

def delay_table():
    frequency = FBASE + jnp.arange(NF, dtype=jnp.int32)[:, None]
    delays = jnp.arange(LAGS, dtype=jnp.int32)[None, :] - LAGS // 2
    angles = 2.0 * math.pi * (frequency * delays % NSEG).astype(jnp.float32) / NSEG
    return jnp.concatenate([jnp.cos(angles), -jnp.sin(angles)], axis=0).astype(jnp.bfloat16)

def whiten(spectrum):
    real_part = spectrum[:, :NF]
    imag_part = spectrum[:, NF:]
    power = real_part * real_part + imag_part * imag_part
    average = lax.optimization_barrier(jnp.mean(power, axis=1, keepdims=True))
    factor = lax.rsqrt(power + 0.1 * average + 1e-05)
    return jnp.concatenate([real_part * factor, imag_part * factor], axis=1).astype(jnp.bfloat16)

def correlate(chosen, receivers, delays):
    source_real = chosen[..., :NF].astype(jnp.float32)
    source_imag = chosen[..., NF:].astype(jnp.float32)
    recv_real = receivers[..., :NF].astype(jnp.float32)
    recv_imag = receivers[..., NF:].astype(jnp.float32)
    cross_real = jnp.einsum('swf,rwf->srf', source_real, recv_real) + jnp.einsum('swf,rwf->srf', source_imag, recv_imag)
    cross_imag = jnp.einsum('swf,rwf->srf', source_imag, recv_real) - jnp.einsum('swf,rwf->srf', source_real, recv_imag)
    cross = jnp.concatenate([cross_real, cross_imag], axis=2).astype(jnp.bfloat16)
    source_count = chosen.shape[0]
    recv_count = receivers.shape[0]
    lagged = jnp.dot(cross.reshape(source_count * recv_count, 2 * NF), delays, preferred_element_type=jnp.float32)
    lagged = lagged.reshape(source_count, recv_count, LAGS) * (1.0 / math.sqrt(SEGS * NF))
    return lagged.astype(jnp.bfloat16)

def reference(recording, source_index, channel_mask):
    padded = jnp.pad(recording, ((0, 0), (TAPS - 4, 0)))
    decimated = decimate(padded, lowpass_taps(), NT)
    spectrum = jnp.dot(decimated.reshape(CHANNELS * SEGS, NSEG), fourier_table(), preferred_element_type=jnp.float32)
    whitened = whiten(spectrum).reshape(CHANNELS, SEGS, 2 * NF)
    whitened = whitened * channel_mask.astype(jnp.bfloat16)[:, None, None]
    chosen = jnp.take(whitened, source_index.astype(jnp.int32), axis=0)
    delays = delay_table()
    blocks = whitened.reshape(N_CHAN, CH_DEV, SEGS, 2 * NF)

    def one_group(receivers):
        return correlate(chosen, receivers, delays)
    result = lax.map(one_group, blocks)
    return result.transpose(1, 0, 2, 3).reshape(SOURCES, CHANNELS, LAGS)
```

```python
import functools
import math

import jax
import jax.numpy as jnp
import ml_dtypes
import numpy as np
from jax import lax
from jax.experimental import pallas as pl
from jax.experimental.pallas import tpu as pltpu
from jax.sharding import PartitionSpec as P

SEGS = 8
NSEG = 512
NF = 192
FBASE = 4
LAGS = 256
TAPS = 64
SOURCES = 512


def from_behind(block, axis, distance):
    devices = range(lax.axis_size(axis))
    route = [(i - distance, i) for i in devices if i - distance in devices]
    return lax.ppermute(block, axis, route)


def lowpass_taps():
    offsets = jnp.arange(TAPS, dtype=jnp.float32) - (TAPS - 1) / 2.0
    cutoff = 0.1
    window = 0.5 - 0.5 * jnp.cos(2.0 * math.pi * (jnp.arange(TAPS, dtype=jnp.float32) + 0.5) / TAPS)
    kernel = 2.0 * cutoff * jnp.sinc(2.0 * cutoff * offsets) * window
    kernel = kernel / jnp.sum(kernel)
    return kernel[::-1].astype(jnp.bfloat16)


def decimate(padded, reversed_taps, out_length):
    summed = jnp.zeros((padded.shape[0], out_length), jnp.float32)
    for stride in range(TAPS // 4):
        window_rows = padded[:, 4 * stride : 4 * stride + 4 * out_length].reshape(
            padded.shape[0], out_length, 4
        )
        weights = reversed_taps[4 * stride : 4 * stride + 4]
        summed = summed + jnp.einsum(
            "ctq,q->ct", window_rows, weights, preferred_element_type=jnp.float32
        )
    return summed.astype(jnp.bfloat16)


def fourier_table():
    sample = jnp.arange(NSEG, dtype=jnp.int32)[:, None]
    frequency = FBASE + jnp.arange(NF, dtype=jnp.int32)[None, :]
    angles = 2.0 * math.pi * (sample * frequency % NSEG).astype(jnp.float32) / NSEG
    return jnp.concatenate([jnp.cos(angles), -jnp.sin(angles)], axis=1).astype(jnp.bfloat16)


def delay_table():
    frequency = FBASE + jnp.arange(NF, dtype=jnp.int32)[:, None]
    delays = jnp.arange(LAGS, dtype=jnp.int32)[None, :] - LAGS // 2
    angles = 2.0 * math.pi * (frequency * delays % NSEG).astype(jnp.float32) / NSEG
    return jnp.concatenate([jnp.cos(angles), -jnp.sin(angles)], axis=0).astype(jnp.bfloat16)


def whiten(spectrum):
    real_part = spectrum[:, :NF]
    imag_part = spectrum[:, NF:]
    power = real_part * real_part + imag_part * imag_part
    average = jnp.mean(power, axis=1, keepdims=True)
    factor = lax.rsqrt(power + 0.1 * average + 1e-05)
    return jnp.concatenate([real_part * factor, imag_part * factor], axis=1).astype(jnp.bfloat16)


def correlate(chosen, receivers, delays):
    source_real = chosen[..., :NF]
    source_imag = chosen[..., NF:]
    recv_real = receivers[..., :NF]
    recv_imag = receivers[..., NF:]
    cross_real = jnp.einsum(
        "swf,rwf->srf", source_real, recv_real, preferred_element_type=jnp.float32
    )
    cross_real = cross_real + jnp.einsum(
        "swf,rwf->srf", source_imag, recv_imag, preferred_element_type=jnp.float32
    )
    cross_imag = jnp.einsum(
        "swf,rwf->srf", source_imag, recv_real, preferred_element_type=jnp.float32
    )
    cross_imag = cross_imag - jnp.einsum(
        "swf,rwf->srf", source_real, recv_imag, preferred_element_type=jnp.float32
    )
    cross = jnp.concatenate([cross_real, cross_imag], axis=2).astype(jnp.bfloat16)
    source_count = chosen.shape[0]
    recv_count = receivers.shape[0]
    lagged = jnp.dot(
        cross.reshape(source_count * recv_count, 2 * NF), delays, preferred_element_type=jnp.float32
    )
    lagged = lagged.reshape(source_count, recv_count, LAGS) * (1.0 / math.sqrt(SEGS * NF))
    return lagged.astype(jnp.bfloat16)


def body(recording, source_index, channel_mask):
    channels, raw_count = recording.shape
    devices = lax.axis_size("chan")
    per_device = channels // devices
    dec_length = raw_count // 4
    trailing = recording[:, raw_count - (TAPS - 4) :]
    earlier = from_behind(trailing, "chan", 1)
    padded = jnp.concatenate([earlier, recording], axis=1)
    decimated = decimate(padded, lowpass_taps(), dec_length)
    grouped = decimated.reshape(devices, per_device, dec_length)
    fourier = fourier_table()
    block = lax.all_to_all(grouped, "chan", split_axis=0, concat_axis=2, tiled=True)
    members = block.shape[1]
    segments = block.reshape(members * SEGS, NSEG)
    spectrum = jnp.dot(segments, fourier, preferred_element_type=jnp.float32)
    whitened = whiten(spectrum).reshape(members, SEGS, 2 * NF)
    whitened = whitened * channel_mask.astype(jnp.bfloat16)[:, None, None]
    initial = jnp.zeros((SOURCES, SEGS, 2 * NF), jnp.bfloat16)
    shard_rows = lax.all_gather(whitened, "chan", axis=0, tiled=True)
    row_count = shard_rows.shape[0]
    inside = (source_index >= 0) & (source_index < row_count)
    picked_rows = jnp.take(shard_rows, jnp.clip(source_index, 0, row_count - 1), axis=0)
    chosen = jnp.where(inside[:, None, None], picked_rows, initial)
    delays = delay_table()

    def one_block(chosen_block):
        return correlate(chosen_block, whitened, delays)

    blocks = chosen.reshape(4, SOURCES // 4, SEGS, 2 * NF)
    result = lax.map(one_block, blocks)
    return result.reshape(SOURCES, per_device, LAGS)


CHIPS = SEGS
TAIL = 128
GROUP = 16
GROUPS = NF // GROUP
FLAG_ROWS = 16
ROWS = 2 * NF + FLAG_ROWS
CHUNKS = ((0, 112), (112, 96), (208, 96), (304, 96))
MIB = 1024 * 1024


def numpy_taps():
    k = np.arange(TAPS, dtype=np.float64)
    window = 0.5 - 0.5 * np.cos(2.0 * np.pi * (k + 0.5) / TAPS)
    taps = 0.2 * np.sinc(0.2 * (k - (TAPS - 1) / 2.0)) * window
    return (taps / taps.sum()).astype(ml_dtypes.bfloat16)


def decimation_tables(raw_count):
    taps = numpy_taps()
    n = np.arange(raw_count // 4)[None, :]

    def table(position):
        k = 4 * n + 3 - position[:, None]
        return np.where((k >= 0) & (k < TAPS), taps[np.clip(k, 0, TAPS - 1)], 0).astype(ml_dtypes.bfloat16)

    return table(np.arange(raw_count)), table(np.arange(-TAIL, 0))


def numpy_fourier():
    frequency = FBASE + np.arange(NF)[:, None]
    angles = 2.0 * np.pi * (frequency * np.arange(NSEG)[None, :] % NSEG) / NSEG
    return np.concatenate([np.cos(angles), -np.sin(angles)], axis=0).astype(ml_dtypes.bfloat16)


def numpy_delays():
    frequency = FBASE + np.arange(NF)[:, None]
    delays = np.arange(LAGS)[None, :] - LAGS // 2
    angles = 2.0 * np.pi * (frequency * delays % NSEG) / NSEG
    pair = np.stack([np.cos(angles), -np.sin(angles)]).reshape(2, GROUPS, GROUP, LAGS)
    return pair.transpose(1, 0, 2, 3).reshape(2 * NF, LAGS).astype(ml_dtypes.bfloat16)


def table_rows(raw_count):
    ends = np.cumsum([0, raw_count, TAIL, 2 * NF, 2 * NF, 2 * NF])
    return [slice(int(a), int(b)) for a, b in zip(ends[:-1], ends[1:])]


def chip_at(place):
    upper = place // (CHIPS // 2)
    return (1 - upper) * 2 * place + upper * (2 * CHIPS - 1 - 2 * place)


def spectra_kernel(
    x_ref, flags_ref, table_ref, g_ref, xs, halo,
    own_sem, pair_send, pair_recv, halo_send, halo_recv, ring_send, ring_recv, side_send, side_recv,
):
    me = lax.axis_index("chan")
    core = lax.rem(me, 2)
    chip = me // 2
    z = chip // 2
    y = lax.rem(chip, 2)
    place = z + y * (CHIPS - 1 - 2 * z)
    forward = chip_at(lax.rem(place + 1, CHIPS)) * 2 + core
    backward = chip_at(lax.rem(place + CHIPS - 1, CHIPS)) * 2 + core
    sibling = chip * 2 + 1 - core
    half = x_ref.shape[0] // 2
    raw_count = x_ref.shape[1]
    gives_halo = jnp.logical_and(core == 1, chip < CHIPS - 1)
    takes_halo = chip > 0

    own = pltpu.make_async_copy(x_ref.at[pl.ds(core * half, half), :], xs.at[core], own_sem)
    own.start()
    barrier = pltpu.get_barrier_semaphore()

    def greet(device):
        pl.semaphore_signal(barrier, inc=1, device_id={"chan": device}, device_id_type=pl.DeviceIdType.MESH)

    for device in (sibling, forward, backward):
        greet(device)

    @pl.when(takes_halo)
    def _():
        greet(me - core - 1)

    @pl.when(gives_halo)
    def _():
        greet(me + 1)
        greet(me + 2)

    pl.semaphore_wait(barrier, 3 + jnp.where(takes_halo, 1, 0) + jnp.where(gives_halo, 2, 0))

    def send(source, target, send_sem, recv_sem, device):
        return pltpu.make_async_remote_copy(
            src_ref=source, dst_ref=target, send_sem=send_sem, recv_sem=recv_sem,
            device_id={"chan": device}, device_id_type=pl.DeviceIdType.MESH,
        )

    def halo_copy(h):
        return send(
            x_ref.at[pl.ds(h * half, half), pl.ds(raw_count - TAIL, TAIL)], halo,
            halo_send.at[h], halo_recv, me + 1 + h,
        )

    @pl.when(gives_halo)
    def _():
        halo_copy(0).start()
        halo_copy(1).start()

    pair = send(
        x_ref.at[pl.ds((1 - core) * half, half), :], xs.at[core], pair_send, pair_recv, sibling
    )
    pair.start()

    @pl.when(chip == 0)
    def _():
        halo[...] = jnp.zeros_like(halo)

    @pl.when(takes_halo)
    def _():
        halo_copy(0).wait_recv()

    own.wait()
    pair_in = send(x_ref.at[pl.ds(0, half), :], xs.at[1 - core], pair_send, pair_recv, sibling)
    pair_in.wait_recv()

    def product(a, b):
        return jnp.dot(a, b, preferred_element_type=jnp.float32)

    block, tail, before, after, _ = table_rows(raw_count)
    first = product(xs[0], table_ref[block]) + product(halo[...], table_ref[tail])
    second = product(xs[1], table_ref[block]) + product(xs[0, :, raw_count - TAIL :], table_ref[tail])

    def transform(table, decimated):
        return lax.dot_general(
            table, decimated.astype(jnp.bfloat16), (((1,), (1,)), ((), ())), preferred_element_type=jnp.float32
        )

    spectrum = transform(table_ref[before], first) + transform(table_ref[after], second)
    real_part = spectrum[:NF]
    imag_part = spectrum[NF:]
    power = real_part * real_part + imag_part * imag_part
    average = jnp.mean(power, axis=0, keepdims=True)
    factor = lax.rsqrt(power + 0.1 * average + 1e-05)
    g_ref[me, 0:NF, :] = (real_part * factor).astype(jnp.bfloat16)
    g_ref[me, NF : 2 * NF, :] = (imag_part * factor).astype(jnp.bfloat16)
    g_ref[me, 2 * NF : ROWS, :] = flags_ref[...]

    def piece(distance, c, side):
        device = chip_at(lax.rem(place + CHIPS - distance, CHIPS)) * 2 + side
        return g_ref.at[device, pl.ds(CHUNKS[c][0], CHUNKS[c][1]), :]

    def onward(way, step, c):
        view = piece(step if way == 0 else (CHIPS - step) % CHIPS, c, core)
        return send(
            view, view, ring_send.at[way, step, c], ring_recv.at[way, step, c], backward if way else forward
        )

    def across(distance, c, side):
        view = piece(distance, c, side)
        return send(view, view, side_send.at[distance, c], side_recv.at[distance, c], sibling)

    last = CHIPS // 2 - 1
    count = len(CHUNKS)
    moves = [
        [(way, c) for c in range(count) for way in range(2) if step < last or way == c // (count // 2)]
        for step in range(last + 1)
    ]
    for way, c in moves[0]:
        onward(way, 0, c).start()
    for c in range(count):
        across(0, c, core).start()
    for step in range(last + 1):
        for way, c in moves[step]:
            distance = step + 1 if way == 0 else CHIPS - step - 1
            view = piece(distance, c, core)
            send(view, view, ring_send.at[way, step, c], ring_recv.at[way, step, c], forward).wait_recv()
            if step < last and (way, c) in moves[step + 1]:
                onward(way, step + 1, c).start()
            across(distance, c, core).start()
    for step in range(last + 1):
        for way, c in moves[step]:
            onward(way, step, c).wait_send()
    for distance in range(CHIPS):
        for c in range(count):
            across(distance, c, core).wait_send()
            across(distance, c, 1 - core).wait_recv()
    pair.wait_send()

    @pl.when(gives_halo)
    def _():
        halo_copy(0).wait_send()
        halo_copy(1).wait_send()


def correlate_kernel(
    delays, me_ref, index_ref, g_ref, table_ref, out_ref, weights, cross, mixed, result, out_sem
):
    half = g_ref.shape[2]
    blocks, sources, receivers, _ = result.shape
    side = mixed.shape[2] // sources
    flags = g_ref[0, 2 * NF : ROWS, :].astype(jnp.float32)
    for device in range(1, 2 * CHIPS):
        flags = flags + g_ref[device, 2 * NF : ROWS, :].astype(jnp.float32)
    flags = [flags[h : h + 1, :].astype(jnp.bfloat16) for h in range(2)]

    def spectra(group, h):
        parts = [
            g_ref[2 * w + h, c * NF + group * GROUP : c * NF + (group + 1) * GROUP, :]
            for c in range(2)
            for w in range(SEGS)
        ]
        return jnp.concatenate(parts, axis=0) * flags[h]

    def chooser(h, wanted, shape, axis):
        channel = lax.broadcasted_iota(jnp.int32, shape, axis) + h * half
        return jnp.where(channel == wanted, 1.0, 0.0).astype(jnp.bfloat16)

    mine = lax.broadcasted_iota(jnp.int32, (receivers, half), 0) + me_ref[0] * receivers
    pick = [chooser(h, mine, (receivers, half), 1) for h in range(2)]
    width = 2 * SEGS * GROUP
    lane = lax.broadcasted_iota(jnp.int32, (GROUP, width), 1)
    same = lax.rem(lane, GROUP) == lax.broadcasted_iota(jnp.int32, (GROUP, width), 0)
    same = jnp.where(same, 1.0, 0.0)[None]
    for group in range(GROUPS):
        rows = jnp.zeros((receivers, width), jnp.float32)
        for h in range(2):
            rows = rows + lax.dot_general(
                pick[h], spectra(group, h), (((1,), (1,)), ((), ())), preferred_element_type=jnp.float32
            )
        turned = jnp.concatenate([-rows[:, width // 2 :], rows[:, : width // 2]], axis=1)
        weights[group, :, 0:GROUP, :] = (rows[:, None, :] * same).astype(jnp.bfloat16)
        weights[group, :, GROUP : 2 * GROUP, :] = (turned[:, None, :] * same).astype(jnp.bfloat16)

    def write(at, part):
        return pltpu.make_async_copy(
            result.at[at, :, pl.ds(part * side, side), :],
            out_ref.at[pl.ds(at * sources, sources), pl.ds(part * side, side), :],
            out_sem.at[at, part],
        )

    def one_block(at, carry):
        wanted = index_ref[:, pl.ds(pl.multiple_of(at * sources, sources), sources)]
        chosen_by = [chooser(h, wanted, (half, sources), 0) for h in range(2)]
        part = 8
        for group in range(GROUPS):
            chosen = jnp.zeros((width, sources), jnp.float32)
            for h in range(2):
                chosen = chosen + jnp.dot(spectra(group, h), chosen_by[h], preferred_element_type=jnp.float32)
            chosen = chosen.astype(jnp.bfloat16)
            for r in range(0, receivers, part):
                block = weights[group, r : r + part].reshape(part * 2 * GROUP, width)
                product = jnp.dot(block, chosen, preferred_element_type=jnp.float32)
                cross[r : r + part, group * 2 * GROUP : (group + 1) * 2 * GROUP, :] = product.astype(
                    jnp.bfloat16
                ).reshape(part, 2 * GROUP, sources)
        for r in range(receivers):
            lagged = lax.dot_general(
                cross[r], table_ref[delays], (((0,), (0,)), ((), ())), preferred_element_type=jnp.float32
            )
            slot = r // side % 2
            for l in range(0, LAGS, 128):
                mixed[slot, l // 128, pl.ds(r % side, sources, stride=side), :] = lagged[:, l : l + 128] * (
                    1.0 / math.sqrt(SEGS * NF)
                )
            if r % side == side - 1:
                for l in range(0, LAGS, 128):
                    done = mixed[slot, l // 128].reshape(sources, side, 128).astype(jnp.bfloat16)
                    result[at, :, r - side + 1 : r + 1, l : l + 128] = done
                write(at, r // side).start()
        return carry

    lax.fori_loop(0, blocks, one_block, 0)
    for at in range(blocks):
        for part in range(receivers // side):
            write(at, part).wait()


def fast_body(recording, source_index, channel_mask):
    channels, raw_count = recording.shape
    half = channels // 2
    per_device = channel_mask.shape[0]
    me = lax.axis_index("chan")
    spread = jnp.tile(channel_mask, channels // per_device)
    mine = jnp.arange(channels, dtype=jnp.int32) // per_device == me
    flags = jnp.where(mine, spread, 0).astype(jnp.bfloat16).reshape(2, half)
    flags = jnp.pad(flags, ((0, FLAG_ROWS - 2), (0, 0)))
    block_table, tail_table = decimation_tables(raw_count)
    fourier = numpy_fourier()
    tables = [block_table, tail_table, fourier[:, : NSEG // 2], fourier[:, NSEG // 2 :], numpy_delays()]
    tables = jnp.asarray(np.concatenate(tables))
    vmem = pl.BlockSpec(memory_space=pltpu.VMEM)
    hbm = pl.BlockSpec(memory_space=pltpu.HBM)
    dma = pltpu.SemaphoreType.DMA
    bf16 = jnp.bfloat16
    count = len(CHUNKS)
    gathered = pl.pallas_call(
        spectra_kernel,
        out_shape=jax.ShapeDtypeStruct((2 * CHIPS, ROWS, half), jnp.bfloat16),
        in_specs=[hbm, vmem, vmem],
        out_specs=vmem,
        scratch_shapes=[
            pltpu.VMEM((2, half, raw_count), jnp.bfloat16),
            pltpu.VMEM((half, TAIL), jnp.bfloat16),
            dma, dma, dma, dma((2,)), dma,
            dma((2, CHIPS // 2, count)), dma((2, CHIPS // 2, count)), dma((CHIPS, count)), dma((CHIPS, count)),
        ],
        compiler_params=pltpu.CompilerParams(
            collective_id=0, has_side_effects=True, vmem_limit_bytes=24 * MIB
        ),
        name="spectra",
    )(recording, flags, tables)
    sources = source_index.shape[0]
    block = 256
    receivers = per_device
    blocks = sources // block
    side = 16
    return pl.pallas_call(
        functools.partial(correlate_kernel, table_rows(raw_count)[-1]),
        out_shape=jax.ShapeDtypeStruct((sources, receivers, LAGS), bf16),
        in_specs=[pl.BlockSpec(memory_space=pltpu.SMEM), vmem, vmem, vmem],
        out_specs=hbm,
        scratch_shapes=[
            pltpu.VMEM((GROUPS, receivers, 2 * GROUP, 2 * SEGS * GROUP), bf16),
            pltpu.VMEM((receivers, 2 * NF, block), bf16),
            pltpu.VMEM((2, LAGS // 128, block * side, 128), jnp.float32),
            pltpu.VMEM((blocks, block, receivers, LAGS), bf16),
            dma((blocks, receivers // side)),
        ],
        compiler_params=pltpu.CompilerParams(vmem_limit_bytes=44 * MIB),
        name="correlate",
    )(me.reshape(1), source_index.reshape(1, sources), gathered, tables)


def solution(mesh):
    placed = (P("fiber", "chan"), P("fiber"), P(("fiber", "chan")))
    chosen_body = fast_body if mesh.shape["chan"] == 2 * SEGS else body
    return jax.shard_map(
        chosen_body, mesh=mesh, in_specs=placed, out_specs=P("fiber", "chan", None), check_vma=False
    )
```

```python
import math

import jax
import jax.numpy as jnp
import ml_dtypes
import numpy as np
from jax import lax
from jax.experimental import pallas as pl
from jax.experimental.pallas import tpu as pltpu
from jax.sharding import PartitionSpec as P

SEGS = 8
NSEG = 512
NF = 192
FBASE = 4
LAGS = 256
TAPS = 64
SOURCES = 512


def from_behind(block, axis, distance):
    devices = range(lax.axis_size(axis))
    route = [(i - distance, i) for i in devices if i - distance in devices]
    return lax.ppermute(block, axis, route)


def lowpass_taps():
    offsets = jnp.arange(TAPS, dtype=jnp.float32) - (TAPS - 1) / 2.0
    cutoff = 0.1
    window = 0.5 - 0.5 * jnp.cos(2.0 * math.pi * (jnp.arange(TAPS, dtype=jnp.float32) + 0.5) / TAPS)
    kernel = 2.0 * cutoff * jnp.sinc(2.0 * cutoff * offsets) * window
    kernel = kernel / jnp.sum(kernel)
    return kernel[::-1].astype(jnp.bfloat16)


def decimate(padded, reversed_taps, out_length):
    summed = jnp.zeros((padded.shape[0], out_length), jnp.float32)
    for stride in range(TAPS // 4):
        window_rows = padded[:, 4 * stride : 4 * stride + 4 * out_length].reshape(
            padded.shape[0], out_length, 4
        )
        weights = reversed_taps[4 * stride : 4 * stride + 4]
        summed = summed + jnp.einsum(
            "ctq,q->ct", window_rows, weights, preferred_element_type=jnp.float32
        )
    return summed.astype(jnp.bfloat16)


def fourier_table():
    sample = jnp.arange(NSEG, dtype=jnp.int32)[:, None]
    frequency = FBASE + jnp.arange(NF, dtype=jnp.int32)[None, :]
    angles = 2.0 * math.pi * (sample * frequency % NSEG).astype(jnp.float32) / NSEG
    return jnp.concatenate([jnp.cos(angles), -jnp.sin(angles)], axis=1).astype(jnp.bfloat16)


def delay_table():
    frequency = FBASE + jnp.arange(NF, dtype=jnp.int32)[:, None]
    delays = jnp.arange(LAGS, dtype=jnp.int32)[None, :] - LAGS // 2
    angles = 2.0 * math.pi * (frequency * delays % NSEG).astype(jnp.float32) / NSEG
    return jnp.concatenate([jnp.cos(angles), -jnp.sin(angles)], axis=0).astype(jnp.bfloat16)


def whiten(spectrum):
    real_part = spectrum[:, :NF]
    imag_part = spectrum[:, NF:]
    power = real_part * real_part + imag_part * imag_part
    average = jnp.mean(power, axis=1, keepdims=True)
    factor = lax.rsqrt(power + 0.1 * average + 1e-05)
    return jnp.concatenate([real_part * factor, imag_part * factor], axis=1).astype(jnp.bfloat16)


def correlate(chosen, receivers, delays):
    source_real = chosen[..., :NF]
    source_imag = chosen[..., NF:]
    recv_real = receivers[..., :NF]
    recv_imag = receivers[..., NF:]
    cross_real = jnp.einsum(
        "swf,rwf->srf", source_real, recv_real, preferred_element_type=jnp.float32
    )
    cross_real = cross_real + jnp.einsum(
        "swf,rwf->srf", source_imag, recv_imag, preferred_element_type=jnp.float32
    )
    cross_imag = jnp.einsum(
        "swf,rwf->srf", source_imag, recv_real, preferred_element_type=jnp.float32
    )
    cross_imag = cross_imag - jnp.einsum(
        "swf,rwf->srf", source_real, recv_imag, preferred_element_type=jnp.float32
    )
    cross = jnp.concatenate([cross_real, cross_imag], axis=2).astype(jnp.bfloat16)
    source_count = chosen.shape[0]
    recv_count = receivers.shape[0]
    lagged = jnp.dot(
        cross.reshape(source_count * recv_count, 2 * NF), delays, preferred_element_type=jnp.float32
    )
    lagged = lagged.reshape(source_count, recv_count, LAGS) * (1.0 / math.sqrt(SEGS * NF))
    return lagged.astype(jnp.bfloat16)


def body(recording, source_index, channel_mask):
    channels, raw_count = recording.shape
    devices = lax.axis_size("chan")
    per_device = channels // devices
    dec_length = raw_count // 4
    trailing = recording[:, raw_count - (TAPS - 4) :]
    earlier = from_behind(trailing, "chan", 1)
    padded = jnp.concatenate([earlier, recording], axis=1)
    decimated = decimate(padded, lowpass_taps(), dec_length)
    grouped = decimated.reshape(devices, per_device, dec_length)
    fourier = fourier_table()
    block = lax.all_to_all(grouped, "chan", split_axis=0, concat_axis=2, tiled=True)
    members = block.shape[1]
    segments = block.reshape(members * SEGS, NSEG)
    spectrum = jnp.dot(segments, fourier, preferred_element_type=jnp.float32)
    whitened = whiten(spectrum).reshape(members, SEGS, 2 * NF)
    whitened = whitened * channel_mask.astype(jnp.bfloat16)[:, None, None]
    initial = jnp.zeros((SOURCES, SEGS, 2 * NF), jnp.bfloat16)
    shard_rows = lax.all_gather(whitened, "chan", axis=0, tiled=True)
    row_count = shard_rows.shape[0]
    inside = (source_index >= 0) & (source_index < row_count)
    picked_rows = jnp.take(shard_rows, jnp.clip(source_index, 0, row_count - 1), axis=0)
    chosen = jnp.where(inside[:, None, None], picked_rows, initial)
    delays = delay_table()

    def one_block(chosen_block):
        return correlate(chosen_block, whitened, delays)

    blocks = chosen.reshape(4, SOURCES // 4, SEGS, 2 * NF)
    result = lax.map(one_block, blocks)
    return result.reshape(SOURCES, per_device, LAGS)


CHIPS = SEGS
TAIL = 128
GROUP = 16
GROUPS = NF // GROUP
FLAG_ROWS = 16
QUAD = 4
ROWS = 2 * NF + FLAG_ROWS
CHUNKS = ((0, 112), (112, 96), (208, 96), (304, 96))
MIB = 1024 * 1024


def numpy_taps():
    k = np.arange(TAPS, dtype=np.float64)
    window = 0.5 - 0.5 * np.cos(2.0 * np.pi * (k + 0.5) / TAPS)
    taps = 0.2 * np.sinc(0.2 * (k - (TAPS - 1) / 2.0)) * window
    return (taps / taps.sum()).astype(ml_dtypes.bfloat16)


def decimation_tables(raw_count):
    taps = numpy_taps()
    n = np.arange(raw_count // 4)[None, :]

    def table(position):
        k = 4 * n + 3 - position[:, None]
        return np.where((k >= 0) & (k < TAPS), taps[np.clip(k, 0, TAPS - 1)], 0).astype(ml_dtypes.bfloat16)

    return table(np.arange(raw_count)), table(np.arange(-TAIL, 0))


def numpy_fourier():
    frequency = FBASE + np.arange(NF)[:, None]
    angles = 2.0 * np.pi * (frequency * np.arange(NSEG)[None, :] % NSEG) / NSEG
    return np.concatenate([np.cos(angles), -np.sin(angles)], axis=0).astype(ml_dtypes.bfloat16)


def numpy_delays():
    frequency = FBASE + np.arange(NF)[:, None]
    delays = np.arange(LAGS)[None, :] - LAGS // 2
    angles = 2.0 * np.pi * (frequency * delays % NSEG) / NSEG
    pair = np.stack([np.cos(angles), -np.sin(angles)]).reshape(2, GROUPS, GROUP, LAGS).transpose(1, 0, 2, 3)
    slot = np.arange(GROUPS)
    order = [slot // QUAD * QUAD + (slot - a) % QUAD for a in range(QUAD)]
    return np.concatenate([pair[at].reshape(2 * NF, LAGS) for at in order]).astype(ml_dtypes.bfloat16)


def table_rows(raw_count):
    ends = np.cumsum([0, raw_count, TAIL, 2 * NF, 2 * NF])
    return [slice(int(a), int(b)) for a, b in zip(ends[:-1], ends[1:])]


def chip_at(place):
    upper = place // (CHIPS // 2)
    return (1 - upper) * 2 * place + upper * (2 * CHIPS - 1 - 2 * place)


def spectra_kernel(
    x_ref, flags_ref, table_ref, g_ref, xs, halo,
    own_sem, pair_send, pair_recv, halo_send, halo_recv, ring_send, ring_recv, side_send, side_recv,
):
    me = lax.axis_index("chan")
    core = lax.rem(me, 2)
    chip = me // 2
    z = chip // 2
    y = lax.rem(chip, 2)
    place = z + y * (CHIPS - 1 - 2 * z)
    forward = chip_at(lax.rem(place + 1, CHIPS)) * 2 + core
    backward = chip_at(lax.rem(place + CHIPS - 1, CHIPS)) * 2 + core
    sibling = chip * 2 + 1 - core
    half = x_ref.shape[0] // 2
    raw_count = x_ref.shape[1]
    gives_halo = jnp.logical_and(core == 1, chip < CHIPS - 1)
    takes_halo = chip > 0

    own = pltpu.make_async_copy(x_ref.at[pl.ds(core * half, half), :], xs.at[core], own_sem)
    own.start()
    barrier = pltpu.get_barrier_semaphore()

    def greet(device):
        pl.semaphore_signal(barrier, inc=1, device_id={"chan": device}, device_id_type=pl.DeviceIdType.MESH)

    for device in (sibling, forward, backward):
        greet(device)

    @pl.when(takes_halo)
    def _():
        greet(me - core - 1)

    @pl.when(gives_halo)
    def _():
        greet(me + 1)
        greet(me + 2)

    pl.semaphore_wait(barrier, 3 + jnp.where(takes_halo, 1, 0) + jnp.where(gives_halo, 2, 0))

    def send(source, target, send_sem, recv_sem, device):
        return pltpu.make_async_remote_copy(
            src_ref=source, dst_ref=target, send_sem=send_sem, recv_sem=recv_sem,
            device_id={"chan": device}, device_id_type=pl.DeviceIdType.MESH,
        )

    def halo_copy(h):
        return send(
            x_ref.at[pl.ds(h * half, half), pl.ds(raw_count - TAIL, TAIL)], halo,
            halo_send.at[h], halo_recv, me + 1 + h,
        )

    @pl.when(gives_halo)
    def _():
        halo_copy(0).start()
        halo_copy(1).start()

    pair = send(
        x_ref.at[pl.ds((1 - core) * half, half), :], xs.at[core], pair_send, pair_recv, sibling
    )
    pair.start()

    @pl.when(chip == 0)
    def _():
        halo[...] = jnp.zeros_like(halo)

    @pl.when(takes_halo)
    def _():
        halo_copy(0).wait_recv()

    own.wait()
    pair_in = send(x_ref.at[pl.ds(0, half), :], xs.at[1 - core], pair_send, pair_recv, sibling)
    pair_in.wait_recv()

    def product(a, b):
        return jnp.dot(a, b, preferred_element_type=jnp.float32)

    block, tail, before, after = table_rows(raw_count)
    first = product(xs[0], table_ref[block]) + product(halo[...], table_ref[tail])
    second = product(xs[1], table_ref[block]) + product(xs[0, :, raw_count - TAIL :], table_ref[tail])

    def transform(table, decimated):
        return lax.dot_general(
            table, decimated.astype(jnp.bfloat16), (((1,), (1,)), ((), ())), preferred_element_type=jnp.float32
        )

    spectrum = transform(table_ref[before], first) + transform(table_ref[after], second)
    real_part = spectrum[:NF]
    imag_part = spectrum[NF:]
    power = real_part * real_part + imag_part * imag_part
    average = jnp.mean(power, axis=0, keepdims=True)
    factor = lax.rsqrt(power + 0.1 * average + 1e-05)
    g_ref[me, 0:NF, :] = (real_part * factor).astype(jnp.bfloat16)
    g_ref[me, NF : 2 * NF, :] = (imag_part * factor).astype(jnp.bfloat16)
    per_device = flags_ref.shape[1]
    to_row = me * per_device // half
    to_lane = me * per_device - to_row * half
    lane = lax.broadcasted_iota(jnp.int32, (per_device, half), 1)
    spot = lane == lax.broadcasted_iota(jnp.int32, (per_device, half), 0) + to_lane
    row = lax.broadcasted_iota(jnp.int32, (FLAG_ROWS, per_device), 0)
    held = jnp.where(row == to_row, flags_ref[...], 0).astype(jnp.float32).astype(jnp.bfloat16)
    placed = product(held, jnp.where(spot, 1.0, 0.0).astype(jnp.bfloat16))
    g_ref[me, 2 * NF : ROWS, :] = placed.astype(jnp.bfloat16)

    def piece(distance, c, side):
        device = chip_at(lax.rem(place + CHIPS - distance, CHIPS)) * 2 + side
        return g_ref.at[device, pl.ds(CHUNKS[c][0], CHUNKS[c][1]), :]

    def onward(way, step, c):
        view = piece(step if way == 0 else (CHIPS - step) % CHIPS, c, core)
        return send(
            view, view, ring_send.at[way, step, c], ring_recv.at[way, step, c], backward if way else forward
        )

    def across(distance, c, side):
        view = piece(distance, c, side)
        return send(view, view, side_send.at[distance, c], side_recv.at[distance, c], sibling)

    last = CHIPS // 2 - 1
    count = len(CHUNKS)
    moves = [
        [(way, c) for c in range(count) for way in range(2) if step < last or way == c // (count // 2)]
        for step in range(last + 1)
    ]
    for way, c in moves[0]:
        onward(way, 0, c).start()
    for c in range(count):
        across(0, c, core).start()
    for step in range(last + 1):
        for way, c in moves[step]:
            distance = step + 1 if way == 0 else CHIPS - step - 1
            view = piece(distance, c, core)
            send(view, view, ring_send.at[way, step, c], ring_recv.at[way, step, c], forward).wait_recv()
            if step < last and (way, c) in moves[step + 1]:
                onward(way, step + 1, c).start()
            across(distance, c, core).start()
    for step in range(last + 1):
        for way, c in moves[step]:
            onward(way, step, c).wait_send()
    for distance in range(CHIPS):
        for c in range(count):
            across(distance, c, core).wait_send()
            across(distance, c, 1 - core).wait_recv()
    pair.wait_send()

    @pl.when(gives_halo)
    def _():
        halo_copy(0).wait_send()
        halo_copy(1).wait_send()


def correlate_kernel(
    me_ref, index_ref, g_ref, table_ref, out_ref, weights, cross, mixed, result, out_sem
):
    half = g_ref.shape[2]
    blocks, sources, receivers, _ = result.shape
    side = mixed.shape[2] // sources
    flags = g_ref[0, 2 * NF : ROWS, :].astype(jnp.float32)
    for device in range(1, 2 * CHIPS):
        flags = flags + g_ref[device, 2 * NF : ROWS, :].astype(jnp.float32)
    flags = [flags[h : h + 1, :].astype(jnp.bfloat16) for h in range(2)]

    def spectra(group, h):
        parts = [
            g_ref[2 * w + h, c * NF + group * GROUP : c * NF + (group + 1) * GROUP, :]
            for c in range(2)
            for w in range(SEGS)
        ]
        return jnp.concatenate(parts, axis=0) * flags[h]

    def chooser(h, wanted, shape, axis):
        channel = lax.broadcasted_iota(jnp.int32, shape, axis) + h * half
        return jnp.where(channel == wanted, 1.0, 0.0).astype(jnp.bfloat16)

    slot = lax.broadcasted_iota(jnp.int32, (receivers, half), 0)
    pick = []
    for turn in range(QUAD):
        mine = slot - lax.rem(slot, QUAD) + lax.rem(slot + QUAD - turn, QUAD) + me_ref[0] * receivers
        pick.append([chooser(h, mine, (receivers, half), 1) for h in range(2)])
    width = 2 * SEGS * GROUP
    lane = lax.broadcasted_iota(jnp.int32, (GROUP, width), 1)
    same = lax.rem(lane, GROUP) == lax.broadcasted_iota(jnp.int32, (GROUP, width), 0)
    same = jnp.where(same, 1.0, 0.0)[None]
    for group in range(GROUPS):
        rows = jnp.zeros((receivers, width), jnp.float32)
        for h in range(2):
            rows = rows + lax.dot_general(
                pick[group % QUAD][h], spectra(group, h), (((1,), (1,)), ((), ())), preferred_element_type=jnp.float32
            )
        turned = jnp.concatenate([-rows[:, width // 2 :], rows[:, : width // 2]], axis=1)
        weights[group, :, 0:GROUP, :] = (rows[:, None, :] * same).astype(jnp.bfloat16)
        weights[group, :, GROUP : 2 * GROUP, :] = (turned[:, None, :] * same).astype(jnp.bfloat16)

    def write(at, part):
        return pltpu.make_async_copy(
            result.at[at, :, pl.ds(part * side, side), :],
            out_ref.at[pl.ds(at * sources, sources), pl.ds(part * side, side), :],
            out_sem.at[at, part],
        )

    def one_block(at, carry):
        wanted = index_ref[:, pl.ds(pl.multiple_of(at * sources, sources), sources)]
        chosen_by = [chooser(h, wanted, (half, sources), 0).astype(jnp.float32).T for h in range(2)]
        chosen_by = [one.astype(jnp.bfloat16) for one in chosen_by]
        part = 2 * QUAD
        quad_lanes = QUAD * 2 * GROUP
        position = lax.rem(
            lax.broadcasted_iota(jnp.int32, (sources, 2 * quad_lanes), 1) // (2 * GROUP), QUAD
        )
        for first in range(0, GROUPS, QUAD):
            chosen = []
            for group in range(first, first + QUAD):
                rows = jnp.zeros((sources, width), jnp.float32)
                for h in range(2):
                    rows = rows + lax.dot_general(
                        chosen_by[h], spectra(group, h), (((1,), (1,)), ((), ())),
                        preferred_element_type=jnp.float32,
                    )
                chosen.append(rows.astype(jnp.bfloat16))
            for r in range(0, receivers, part):
                products = [
                    lax.dot_general(
                        chosen[turn], weights[first + turn, r : r + part].reshape(part * 2 * GROUP, width),
                        (((1,), (1,)), ((), ())), preferred_element_type=jnp.float32,
                    )
                    for turn in range(QUAD)
                ]
                for a in range(QUAD):
                    mixture = products[(QUAD - 1 - a) % QUAD]
                    for j in range(QUAD - 1):
                        mixture = jnp.where(position == j, products[(j - a) % QUAD], mixture)
                    mixture = mixture.astype(jnp.bfloat16)
                    lanes = slice(first * 2 * GROUP, (first + QUAD) * 2 * GROUP)
                    cross[r + a, :, lanes] = mixture[:, :quad_lanes]
                    cross[r + QUAD + a, :, lanes] = mixture[:, quad_lanes:]
        for r in range(receivers):
            delays = slice(r % QUAD * 2 * NF, (r % QUAD + 1) * 2 * NF)
            lagged = jnp.dot(cross[r], table_ref[delays], preferred_element_type=jnp.float32)
            slot = r // side % 2
            for l in range(0, LAGS, 128):
                mixed[slot, l // 128, pl.ds(r % side, sources, stride=side), :] = lagged[:, l : l + 128] * (
                    1.0 / math.sqrt(SEGS * NF)
                )
            if r % side == side - 1:
                for l in range(0, LAGS, 128):
                    done = mixed[slot, l // 128].reshape(sources, side, 128).astype(jnp.bfloat16)
                    result[at, :, r - side + 1 : r + 1, l : l + 128] = done
                write(at, r // side).start()
        return carry

    lax.fori_loop(0, blocks, one_block, 0)
    for at in range(blocks):
        for part in range(receivers // side):
            write(at, part).wait()


def fast_body(recording, source_index, channel_mask):
    channels, raw_count = recording.shape
    half = channels // 2
    per_device = channel_mask.shape[0]
    me = lax.axis_index("chan")
    block_table, tail_table = decimation_tables(raw_count)
    fourier = numpy_fourier()
    tables = [block_table, tail_table, fourier[:, : NSEG // 2], fourier[:, NSEG // 2 :]]
    tables = jnp.asarray(np.concatenate(tables))
    vmem = pl.BlockSpec(memory_space=pltpu.VMEM)
    hbm = pl.BlockSpec(memory_space=pltpu.HBM)
    dma = pltpu.SemaphoreType.DMA
    bf16 = jnp.bfloat16
    count = len(CHUNKS)
    gathered = pl.pallas_call(
        spectra_kernel,
        out_shape=jax.ShapeDtypeStruct((2 * CHIPS, ROWS, half), jnp.bfloat16),
        in_specs=[hbm, vmem, vmem],
        out_specs=vmem,
        scratch_shapes=[
            pltpu.VMEM((2, half, raw_count), jnp.bfloat16),
            pltpu.VMEM((half, TAIL), jnp.bfloat16),
            dma, dma, dma, dma((2,)), dma,
            dma((2, CHIPS // 2, count)), dma((2, CHIPS // 2, count)), dma((CHIPS, count)), dma((CHIPS, count)),
        ],
        compiler_params=pltpu.CompilerParams(
            collective_id=0, has_side_effects=True, vmem_limit_bytes=24 * MIB
        ),
        name="spectra",
    )(recording, channel_mask.reshape(1, per_device), tables)
    sources = source_index.shape[0]
    block = 256
    receivers = per_device
    blocks = sources // block
    side = 16
    return pl.pallas_call(
        correlate_kernel,
        out_shape=jax.ShapeDtypeStruct((sources, receivers, LAGS), bf16),
        in_specs=[pl.BlockSpec(memory_space=pltpu.SMEM), vmem, vmem, vmem],
        out_specs=hbm,
        scratch_shapes=[
            pltpu.VMEM((GROUPS, receivers, 2 * GROUP, 2 * SEGS * GROUP), bf16),
            pltpu.VMEM((receivers, block, 2 * NF), bf16),
            pltpu.VMEM((2, LAGS // 128, block * side, 128), jnp.float32),
            pltpu.VMEM((blocks, block, receivers, LAGS), bf16),
            dma((blocks, receivers // side)),
        ],
        compiler_params=pltpu.CompilerParams(vmem_limit_bytes=44 * MIB),
        name="correlate",
    )(me.reshape(1), source_index.reshape(1, sources), gathered, jnp.asarray(numpy_delays()))


def solution(mesh):
    placed = (P("fiber", "chan"), P("fiber"), P(("fiber", "chan")))
    chosen_body = fast_body if mesh.shape["chan"] == 2 * SEGS else body
    return jax.shard_map(
        chosen_body, mesh=mesh, in_specs=placed, out_specs=P("fiber", "chan", None), check_vma=False
    )
```

```python
import functools
import math

import jax
import jax.numpy as jnp
import ml_dtypes
import numpy as np
from jax import lax
from jax.experimental import pallas as pl
from jax.experimental.pallas import tpu as pltpu
from jax.sharding import PartitionSpec as P

SEGS = 8
NSEG = 512
NF = 192
FBASE = 4
LAGS = 256
TAPS = 64
SOURCES = 512


def from_behind(block, axis, distance):
    devices = range(lax.axis_size(axis))
    route = [(i - distance, i) for i in devices if i - distance in devices]
    return lax.ppermute(block, axis, route)


def lowpass_taps():
    offsets = jnp.arange(TAPS, dtype=jnp.float32) - (TAPS - 1) / 2.0
    cutoff = 0.1
    window = 0.5 - 0.5 * jnp.cos(2.0 * math.pi * (jnp.arange(TAPS, dtype=jnp.float32) + 0.5) / TAPS)
    kernel = 2.0 * cutoff * jnp.sinc(2.0 * cutoff * offsets) * window
    kernel = kernel / jnp.sum(kernel)
    return kernel[::-1].astype(jnp.bfloat16)


def decimate(padded, reversed_taps, out_length):
    summed = jnp.zeros((padded.shape[0], out_length), jnp.float32)
    for stride in range(TAPS // 4):
        window_rows = padded[:, 4 * stride : 4 * stride + 4 * out_length].reshape(
            padded.shape[0], out_length, 4
        )
        weights = reversed_taps[4 * stride : 4 * stride + 4]
        summed = summed + jnp.einsum(
            "ctq,q->ct", window_rows, weights, preferred_element_type=jnp.float32
        )
    return summed.astype(jnp.bfloat16)


def fourier_table():
    sample = jnp.arange(NSEG, dtype=jnp.int32)[:, None]
    frequency = FBASE + jnp.arange(NF, dtype=jnp.int32)[None, :]
    angles = 2.0 * math.pi * (sample * frequency % NSEG).astype(jnp.float32) / NSEG
    return jnp.concatenate([jnp.cos(angles), -jnp.sin(angles)], axis=1).astype(jnp.bfloat16)


def delay_table():
    frequency = FBASE + jnp.arange(NF, dtype=jnp.int32)[:, None]
    delays = jnp.arange(LAGS, dtype=jnp.int32)[None, :] - LAGS // 2
    angles = 2.0 * math.pi * (frequency * delays % NSEG).astype(jnp.float32) / NSEG
    return jnp.concatenate([jnp.cos(angles), -jnp.sin(angles)], axis=0).astype(jnp.bfloat16)


def whiten(spectrum):
    real_part = spectrum[:, :NF]
    imag_part = spectrum[:, NF:]
    power = real_part * real_part + imag_part * imag_part
    average = jnp.mean(power, axis=1, keepdims=True)
    factor = lax.rsqrt(power + 0.1 * average + 1e-05)
    return jnp.concatenate([real_part * factor, imag_part * factor], axis=1).astype(jnp.bfloat16)


def correlate(chosen, receivers, delays):
    source_real = chosen[..., :NF]
    source_imag = chosen[..., NF:]
    recv_real = receivers[..., :NF]
    recv_imag = receivers[..., NF:]
    cross_real = jnp.einsum(
        "swf,rwf->srf", source_real, recv_real, preferred_element_type=jnp.float32
    )
    cross_real = cross_real + jnp.einsum(
        "swf,rwf->srf", source_imag, recv_imag, preferred_element_type=jnp.float32
    )
    cross_imag = jnp.einsum(
        "swf,rwf->srf", source_imag, recv_real, preferred_element_type=jnp.float32
    )
    cross_imag = cross_imag - jnp.einsum(
        "swf,rwf->srf", source_real, recv_imag, preferred_element_type=jnp.float32
    )
    cross = jnp.concatenate([cross_real, cross_imag], axis=2).astype(jnp.bfloat16)
    source_count = chosen.shape[0]
    recv_count = receivers.shape[0]
    lagged = jnp.dot(
        cross.reshape(source_count * recv_count, 2 * NF), delays, preferred_element_type=jnp.float32
    )
    lagged = lagged.reshape(source_count, recv_count, LAGS) * (1.0 / math.sqrt(SEGS * NF))
    return lagged.astype(jnp.bfloat16)


def body(recording, source_index, channel_mask):
    channels, raw_count = recording.shape
    devices = lax.axis_size("chan")
    per_device = channels // devices
    dec_length = raw_count // 4
    trailing = recording[:, raw_count - (TAPS - 4) :]
    earlier = from_behind(trailing, "chan", 1)
    padded = jnp.concatenate([earlier, recording], axis=1)
    decimated = decimate(padded, lowpass_taps(), dec_length)
    grouped = decimated.reshape(devices, per_device, dec_length)
    fourier = fourier_table()
    block = lax.all_to_all(grouped, "chan", split_axis=0, concat_axis=2, tiled=True)
    members = block.shape[1]
    segments = block.reshape(members * SEGS, NSEG)
    spectrum = jnp.dot(segments, fourier, preferred_element_type=jnp.float32)
    whitened = whiten(spectrum).reshape(members, SEGS, 2 * NF)
    whitened = whitened * channel_mask.astype(jnp.bfloat16)[:, None, None]
    initial = jnp.zeros((SOURCES, SEGS, 2 * NF), jnp.bfloat16)
    shard_rows = lax.all_gather(whitened, "chan", axis=0, tiled=True)
    row_count = shard_rows.shape[0]
    inside = (source_index >= 0) & (source_index < row_count)
    picked_rows = jnp.take(shard_rows, jnp.clip(source_index, 0, row_count - 1), axis=0)
    chosen = jnp.where(inside[:, None, None], picked_rows, initial)
    delays = delay_table()

    def one_block(chosen_block):
        return correlate(chosen_block, whitened, delays)

    blocks = chosen.reshape(4, SOURCES // 4, SEGS, 2 * NF)
    result = lax.map(one_block, blocks)
    return result.reshape(SOURCES, per_device, LAGS)


CHIPS = SEGS
TAIL = 128
GROUP = 16
GROUPS = NF // GROUP
FLAG_ROWS = 16
QUAD = 4
ROWS = 2 * NF + FLAG_ROWS
CHUNKS = ((0, 112), (112, 96), (208, 96), (304, 96))
MIB = 1024 * 1024


def numpy_taps():
    k = np.arange(TAPS, dtype=np.float64)
    window = 0.5 - 0.5 * np.cos(2.0 * np.pi * (k + 0.5) / TAPS)
    taps = 0.2 * np.sinc(0.2 * (k - (TAPS - 1) / 2.0)) * window
    return (taps / taps.sum()).astype(ml_dtypes.bfloat16)


def decimation_tables(raw_count):
    taps = numpy_taps()
    n = np.arange(raw_count // 4)[None, :]

    def table(position):
        k = 4 * n + 3 - position[:, None]
        return np.where((k >= 0) & (k < TAPS), taps[np.clip(k, 0, TAPS - 1)], 0).astype(ml_dtypes.bfloat16)

    return table(np.arange(raw_count)), table(np.arange(-TAIL, 0))


def numpy_fourier():
    frequency = FBASE + np.arange(NF)[:, None]
    angles = 2.0 * np.pi * (frequency * np.arange(NSEG)[None, :] % NSEG) / NSEG
    return np.concatenate([np.cos(angles), -np.sin(angles)], axis=0).astype(ml_dtypes.bfloat16)


def numpy_delays():
    frequency = FBASE + np.arange(NF)[:, None]
    delays = np.arange(LAGS)[None, :] - LAGS // 2
    angles = 2.0 * np.pi * (frequency * delays % NSEG) / NSEG
    pair = np.stack([np.cos(angles), -np.sin(angles)]).reshape(2, GROUPS, GROUP, LAGS)
    return pair.transpose(1, 0, 2, 3).reshape(2 * NF, LAGS).astype(ml_dtypes.bfloat16)


def table_rows(raw_count):
    ends = np.cumsum([0, raw_count, TAIL, 2 * NF, 2 * NF, 2 * NF])
    return [slice(int(a), int(b)) for a, b in zip(ends[:-1], ends[1:])]


def chip_at(place):
    upper = place // (CHIPS // 2)
    return (1 - upper) * 2 * place + upper * (2 * CHIPS - 1 - 2 * place)


def spectra_kernel(
    x_ref, flags_ref, table_ref, g_ref, xs, halo,
    own_sem, pair_send, pair_recv, halo_send, halo_recv, ring_send, ring_recv, side_send, side_recv,
):
    me = lax.axis_index("chan")
    core = lax.rem(me, 2)
    chip = me // 2
    z = chip // 2
    y = lax.rem(chip, 2)
    place = z + y * (CHIPS - 1 - 2 * z)
    forward = chip_at(lax.rem(place + 1, CHIPS)) * 2 + core
    backward = chip_at(lax.rem(place + CHIPS - 1, CHIPS)) * 2 + core
    sibling = chip * 2 + 1 - core
    half = x_ref.shape[0] // 2
    raw_count = x_ref.shape[1]
    gives_halo = jnp.logical_and(core == 1, chip < CHIPS - 1)
    takes_halo = chip > 0

    own = pltpu.make_async_copy(x_ref.at[pl.ds(core * half, half), :], xs.at[core], own_sem)
    own.start()
    barrier = pltpu.get_barrier_semaphore()

    def greet(device):
        pl.semaphore_signal(barrier, inc=1, device_id={"chan": device}, device_id_type=pl.DeviceIdType.MESH)

    for device in (sibling, forward, backward):
        greet(device)

    @pl.when(takes_halo)
    def _():
        greet(me - core - 1)

    @pl.when(gives_halo)
    def _():
        greet(me + 1)
        greet(me + 2)

    pl.semaphore_wait(barrier, 3 + jnp.where(takes_halo, 1, 0) + jnp.where(gives_halo, 2, 0))

    def send(source, target, send_sem, recv_sem, device):
        return pltpu.make_async_remote_copy(
            src_ref=source, dst_ref=target, send_sem=send_sem, recv_sem=recv_sem,
            device_id={"chan": device}, device_id_type=pl.DeviceIdType.MESH,
        )

    def halo_copy(h):
        return send(
            x_ref.at[pl.ds(h * half, half), pl.ds(raw_count - TAIL, TAIL)], halo,
            halo_send.at[h], halo_recv, me + 1 + h,
        )

    @pl.when(gives_halo)
    def _():
        halo_copy(0).start()
        halo_copy(1).start()

    pair = send(
        x_ref.at[pl.ds((1 - core) * half, half), :], xs.at[core], pair_send, pair_recv, sibling
    )
    pair.start()

    @pl.when(chip == 0)
    def _():
        halo[...] = jnp.zeros_like(halo)

    @pl.when(takes_halo)
    def _():
        halo_copy(0).wait_recv()

    own.wait()
    pair_in = send(x_ref.at[pl.ds(0, half), :], xs.at[1 - core], pair_send, pair_recv, sibling)
    pair_in.wait_recv()

    def product(a, b):
        return jnp.dot(a, b, preferred_element_type=jnp.float32)

    block, tail, before, after, _ = table_rows(raw_count)
    first = product(xs[0], table_ref[block]) + product(halo[...], table_ref[tail])
    second = product(xs[1], table_ref[block]) + product(xs[0, :, raw_count - TAIL :], table_ref[tail])

    def transform(table, decimated):
        return lax.dot_general(
            table, decimated.astype(jnp.bfloat16), (((1,), (1,)), ((), ())), preferred_element_type=jnp.float32
        )

    spectrum = transform(table_ref[before], first) + transform(table_ref[after], second)
    real_part = spectrum[:NF]
    imag_part = spectrum[NF:]
    power = real_part * real_part + imag_part * imag_part
    average = jnp.mean(power, axis=0, keepdims=True)
    factor = lax.rsqrt(power + 0.1 * average + 1e-05)
    g_ref[me, 0:NF, :] = (real_part * factor).astype(jnp.bfloat16)
    g_ref[me, NF : 2 * NF, :] = (imag_part * factor).astype(jnp.bfloat16)
    per_device = flags_ref.shape[1]
    to_row = me * per_device // half
    to_lane = me * per_device - to_row * half
    lane = lax.broadcasted_iota(jnp.int32, (per_device, half), 1)
    spot = lane == lax.broadcasted_iota(jnp.int32, (per_device, half), 0) + to_lane
    row = lax.broadcasted_iota(jnp.int32, (FLAG_ROWS, per_device), 0)
    held = jnp.where(row == to_row, flags_ref[...], 0).astype(jnp.float32).astype(jnp.bfloat16)
    placed = product(held, jnp.where(spot, 1.0, 0.0).astype(jnp.bfloat16))
    g_ref[me, 2 * NF : ROWS, :] = placed.astype(jnp.bfloat16)

    def piece(distance, c, side):
        device = chip_at(lax.rem(place + CHIPS - distance, CHIPS)) * 2 + side
        return g_ref.at[device, pl.ds(CHUNKS[c][0], CHUNKS[c][1]), :]

    def onward(way, step, c):
        view = piece(step if way == 0 else (CHIPS - step) % CHIPS, c, core)
        return send(
            view, view, ring_send.at[way, step, c], ring_recv.at[way, step, c], backward if way else forward
        )

    def across(distance, c, side):
        view = piece(distance, c, side)
        return send(view, view, side_send.at[distance, c], side_recv.at[distance, c], sibling)

    last = CHIPS // 2 - 1
    count = len(CHUNKS)
    moves = [
        [(way, c) for c in range(count) for way in range(2) if step < last or way == c // (count // 2)]
        for step in range(last + 1)
    ]
    for way, c in moves[0]:
        onward(way, 0, c).start()
    for c in range(count):
        across(0, c, core).start()
    for step in range(last + 1):
        for way, c in moves[step]:
            distance = step + 1 if way == 0 else CHIPS - step - 1
            view = piece(distance, c, core)
            send(view, view, ring_send.at[way, step, c], ring_recv.at[way, step, c], forward).wait_recv()
            if step < last and (way, c) in moves[step + 1]:
                onward(way, step + 1, c).start()
            across(distance, c, core).start()
    for step in range(last + 1):
        for way, c in moves[step]:
            onward(way, step, c).wait_send()
    for distance in range(CHIPS):
        for c in range(count):
            across(distance, c, core).wait_send()
            across(distance, c, 1 - core).wait_recv()
    pair.wait_send()

    @pl.when(gives_halo)
    def _():
        halo_copy(0).wait_send()
        halo_copy(1).wait_send()


def correlate_kernel(
    delays_at, me_ref, index_ref, g_ref, table_ref, out_ref, weights, cross, lagged, turned_delays, result, out_sem
):
    half = g_ref.shape[2]
    blocks, sources, receivers, _ = result.shape
    side = 16
    chunk = 2 * GROUP
    for a in range(QUAD):
        for j in range(GROUPS):
            group = j // QUAD * QUAD + (j - a) % QUAD
            start = delays_at + group * chunk
            turned_delays[a, j * chunk : (j + 1) * chunk, :] = table_ref[start : start + chunk, :]
    to_row = lax.broadcasted_iota(jnp.int32, (side * side, side * side), 0)
    from_row = lax.broadcasted_iota(jnp.int32, (side * side, side * side), 1)
    swap = from_row == lax.rem(to_row, side) * side + to_row // side
    swap = jnp.where(swap, 1.0, 0.0).astype(jnp.bfloat16)
    flags = g_ref[0, 2 * NF : ROWS, :].astype(jnp.float32)
    for device in range(1, 2 * CHIPS):
        flags = flags + g_ref[device, 2 * NF : ROWS, :].astype(jnp.float32)
    flags = [flags[h : h + 1, :].astype(jnp.bfloat16) for h in range(2)]

    def spectra(group, h):
        parts = [
            g_ref[2 * w + h, c * NF + group * GROUP : c * NF + (group + 1) * GROUP, :]
            for c in range(2)
            for w in range(SEGS)
        ]
        return jnp.concatenate(parts, axis=0) * flags[h]

    def chooser(h, wanted, shape, axis):
        channel = lax.broadcasted_iota(jnp.int32, shape, axis) + h * half
        return jnp.where(channel == wanted, 1.0, 0.0).astype(jnp.bfloat16)

    slot = lax.broadcasted_iota(jnp.int32, (receivers, half), 0)
    pick = []
    for turn in range(QUAD):
        mine = slot - lax.rem(slot, QUAD) + lax.rem(slot + QUAD - turn, QUAD) + me_ref[0] * receivers
        pick.append([chooser(h, mine, (receivers, half), 1) for h in range(2)])
    width = 2 * SEGS * GROUP
    lane = lax.broadcasted_iota(jnp.int32, (GROUP, width), 1)
    same = lax.rem(lane, GROUP) == lax.broadcasted_iota(jnp.int32, (GROUP, width), 0)
    same = jnp.where(same, 1.0, 0.0)[None]
    for group in range(GROUPS):
        rows = jnp.zeros((receivers, width), jnp.float32)
        for h in range(2):
            rows = rows + lax.dot_general(
                pick[group % QUAD][h], spectra(group, h), (((1,), (1,)), ((), ())), preferred_element_type=jnp.float32
            )
        turned = jnp.concatenate([-rows[:, width // 2 :], rows[:, : width // 2]], axis=1)
        weights[group, :, 0:GROUP, :] = (rows[:, None, :] * same).astype(jnp.bfloat16)
        weights[group, :, GROUP : 2 * GROUP, :] = (turned[:, None, :] * same).astype(jnp.bfloat16)

    def write(at, part):
        return pltpu.make_async_copy(
            result.at[at, :, pl.ds(part * side, side), :],
            out_ref.at[pl.ds(at * sources, sources), pl.ds(part * side, side), :],
            out_sem.at[at, part],
        )

    def one_block(at, carry):
        wanted = index_ref[:, pl.ds(pl.multiple_of(at * sources, sources), sources)]
        chosen_by = [chooser(h, wanted, (half, sources), 0).astype(jnp.float32).T for h in range(2)]
        chosen_by = [one.astype(jnp.bfloat16) for one in chosen_by]
        part = 2 * QUAD
        quad_lanes = QUAD * 2 * GROUP
        strip = 64
        position = lax.rem(lax.broadcasted_iota(jnp.int32, (strip, 2 * quad_lanes), 1) // (2 * GROUP), QUAD)
        position = position.astype(jnp.float32).astype(jnp.bfloat16)
        for first in range(0, GROUPS, QUAD):
            chosen = []
            for group in range(first, first + QUAD):
                rows = jnp.zeros((sources, width), jnp.float32)
                for h in range(2):
                    rows = rows + lax.dot_general(
                        chosen_by[h], spectra(group, h), (((1,), (1,)), ((), ())),
                        preferred_element_type=jnp.float32,
                    )
                chosen.append(rows.astype(jnp.bfloat16))
            for r in range(0, receivers, part):
                products = [
                    lax.dot_general(
                        chosen[turn], weights[first + turn, r : r + part].reshape(part * 2 * GROUP, width),
                        (((1,), (1,)), ((), ())), preferred_element_type=jnp.float32,
                    ).astype(jnp.bfloat16)
                    for turn in range(QUAD)
                ]
                lanes = slice(first * 2 * GROUP, (first + QUAD) * 2 * GROUP)
                for top in range(0, sources, strip):
                    rows = slice(top, top + strip)
                    strips = [product[rows] for product in products]
                    for a in range(QUAD):
                        mixture = strips[(QUAD - 1 - a) % QUAD]
                        for j in range(QUAD - 1):
                            mixture = jnp.where(position == j, strips[(j - a) % QUAD], mixture)
                        cross[r + a, rows, lanes] = mixture[:, :quad_lanes]
                        cross[r + QUAD + a, rows, lanes] = mixture[:, quad_lanes:]
        for part in range(0, receivers, side):
            for r in range(part, part + side):
                lags = jnp.dot(cross[r], turned_delays[r % QUAD], preferred_element_type=jnp.float32)
                lagged[r] = (lags * (1.0 / math.sqrt(SEGS * NF))).astype(jnp.bfloat16)
            for top in range(0, sources, side):
                tile = lagged[part : part + side, top : top + side, :].reshape(side * side, LAGS)
                tile = jnp.dot(swap, tile, preferred_element_type=jnp.float32).astype(jnp.bfloat16)
                result[at, top : top + side, part : part + side, :] = tile.reshape(side, side, LAGS)
            write(at, part // side).start()
        return carry

    lax.fori_loop(0, blocks, one_block, 0)
    for at in range(blocks):
        for part in range(receivers // side):
            write(at, part).wait()


def fast_body(recording, source_index, channel_mask):
    channels, raw_count = recording.shape
    half = channels // 2
    per_device = channel_mask.shape[0]
    me = lax.axis_index("chan")
    block_table, tail_table = decimation_tables(raw_count)
    fourier = numpy_fourier()
    tables = [block_table, tail_table, fourier[:, : NSEG // 2], fourier[:, NSEG // 2 :], numpy_delays()]
    tables = jnp.asarray(np.concatenate(tables))
    vmem = pl.BlockSpec(memory_space=pltpu.VMEM)
    hbm = pl.BlockSpec(memory_space=pltpu.HBM)
    dma = pltpu.SemaphoreType.DMA
    bf16 = jnp.bfloat16
    count = len(CHUNKS)
    gathered = pl.pallas_call(
        spectra_kernel,
        out_shape=jax.ShapeDtypeStruct((2 * CHIPS, ROWS, half), jnp.bfloat16),
        in_specs=[hbm, vmem, vmem],
        out_specs=vmem,
        scratch_shapes=[
            pltpu.VMEM((2, half, raw_count), jnp.bfloat16),
            pltpu.VMEM((half, TAIL), jnp.bfloat16),
            dma, dma, dma, dma((2,)), dma,
            dma((2, CHIPS // 2, count)), dma((2, CHIPS // 2, count)), dma((CHIPS, count)), dma((CHIPS, count)),
        ],
        compiler_params=pltpu.CompilerParams(
            collective_id=0, has_side_effects=True, vmem_limit_bytes=24 * MIB
        ),
        name="spectra",
    )(recording, channel_mask.reshape(1, per_device), tables)
    sources = source_index.shape[0]
    block = 256
    receivers = per_device
    blocks = sources // block
    side = 16
    return pl.pallas_call(
        functools.partial(correlate_kernel, table_rows(raw_count)[-1].start),
        out_shape=jax.ShapeDtypeStruct((sources, receivers, LAGS), bf16),
        in_specs=[pl.BlockSpec(memory_space=pltpu.SMEM), vmem, vmem, vmem],
        out_specs=hbm,
        scratch_shapes=[
            pltpu.VMEM((GROUPS, receivers, 2 * GROUP, 2 * SEGS * GROUP), bf16),
            pltpu.VMEM((receivers, block, 2 * NF), bf16),
            pltpu.VMEM((receivers, block, LAGS), bf16),
            pltpu.VMEM((QUAD, 2 * NF, LAGS), bf16),
            pltpu.VMEM((blocks, block, receivers, LAGS), bf16),
            dma((blocks, receivers // side)),
        ],
        compiler_params=pltpu.CompilerParams(vmem_limit_bytes=44 * MIB),
        name="correlate",
    )(me.reshape(1), source_index.reshape(1, sources), gathered, tables)


def solution(mesh):
    placed = (P("fiber", "chan"), P("fiber"), P(("fiber", "chan")))
    chosen_body = fast_body if mesh.shape["chan"] == 2 * SEGS else body
    return jax.shard_map(
        chosen_body, mesh=mesh, in_specs=placed, out_specs=P("fiber", "chan", None), check_vma=False
    )
```
